32 devices in a mesh: runs: 2 (over x), patch: 16 (over z, y, core).
Axes of the slice: x: 2, y: 2, z: 4, core: 2. Of those that a mesh axis runs over, the one named last changes fastest.
Arguments:
- depths: float32 [2, 128, 4096], P(None, None, ('runs', 'patch')), parts along dimension 2, may hold values from 0.4 to 1.6
- momenta: float32 [4, 128, 4096], P(None, None, ('runs', 'patch')), parts along dimension 2, may hold values from -1 to 1
- bed: float32 [128, 4096], P(None, ('runs', 'patch')), parts along dimension 1, may hold values from -3 to 3
- active: int32 [1, 32], P(None, ('runs', 'patch')), parts along dimension 1, may hold values from 0 to 1
Outputs:
- new_depths: float32 [2, 128, 4096], P(None, None, ('runs', 'patch')), parts along dimension 2
- new_momenta: float32 [4, 128, 4096], P(None, None, ('runs', 'patch')), parts along dimension 2
The draws below stay inside these ranges and needn't reach their ends.
There are 2 independent parts, one for each index of `runs`. The reference program is written for one: setup_inputs(seed, part) draws one part's arguments, and reference() takes and returns one part's arrays. A program takes and returns all parts, laid end to end along the dimension named above; each array names one. Nothing has to cross between parts.
All inputs are finite; a program needn't handle non-finite values.
Results may differ from the reference program's by a relative error of at most 0.0003.
Values sent between devices are 32-bit elements; how exact they have to be, the bound alone decides.
A program may use at most 64 MiB of HBM per device.

```python
import math
import jax
import jax.numpy as jnp
from jax import lax

PATCH = 128
SLOTS = 1
OUTER = 1
COLUMNS = 16
RAD = 128
AROUND = 2048


def draw_active(key, part):
    key = jax.random.fold_in(key, 11)
    start_key, rest_key, order_key = jax.random.split(key, 3)
    start_column = 2 * jax.random.randint(start_key, (), 0, COLUMNS // 2) + 1
    column_ids = jnp.arange(COLUMNS)
    inside = (column_ids - start_column) % COLUMNS < max(COLUMNS // 4, 2)
    scattered = jax.random.randint(rest_key, (COLUMNS,), 0, 2)
    counts = jnp.where(inside, SLOTS, scattered)
    half_point = COLUMNS // 2
    pinned = (column_ids <= 1) | (column_ids >= COLUMNS - 2) | (column_ids >= half_point - 2) & (column_ids <= half_point + 1)
    counts = jnp.where(pinned, min(2, SLOTS), counts)
    scores = jax.random.randint(order_key, (SLOTS, COLUMNS), 0, 1 << 20) * SLOTS + jnp.arange(SLOTS)[:, None]
    rank_order = jnp.argsort(jnp.argsort(scores, axis=0), axis=0)
    return (rank_order < counts[None, :]).astype(jnp.int32)


def steps_of(stream_key, extent, cuts, least, high):
    level = 1.0
    for axis_at, blocks in cuts:
        steps = jax.random.uniform(jax.random.fold_in(jax.random.fold_in(stream_key, 6), axis_at), (blocks,), jnp.float32, least / len(cuts), high / len(cuts))
        level = level * jnp.repeat(jnp.exp(steps), extent[axis_at] // blocks).reshape((-1,) + (1,) * (len(extent) - 1 - axis_at))
    return level


def noise(key, shape, width, limit, cuts=(), kind=jnp.bfloat16):
    array = width * jax.random.normal(key, shape, jnp.float32)
    if cuts:
        array = array * steps_of(key, shape, cuts, -0.22, 0.18)
    return jnp.clip(array, -limit, limit).astype(kind)


def setup_inputs(seed: int = 0, part: int = 0) -> dict:
    key_list = jax.random.split(jax.random.key(seed), 5)
    part_splits = jax.random.split(jax.random.fold_in(key_list[4], part), 5)
    return {
        "depths": jnp.clip(jnp.exp(math.log(1.6) - 1.3862944 * jax.random.uniform(part_splits[0], (2, RAD, AROUND), jnp.float32) ** steps_of(part_splits[0], (2, RAD, AROUND), ((2, 16),), -0.2, 0.2)), 0.4, 1.6),
        "momenta": noise(part_splits[1], (4, RAD, AROUND), 0.25, 1.0, ((2, 16),), jnp.float32),
        "bed": noise(part_splits[2], (RAD, AROUND), 0.5, 3.0, ((1, 16),), jnp.float32),
        "active": draw_active(jax.random.fold_in(jax.random.fold_in(key_list[4], part), 71), part),
    }


time_step = 0.04
solid_press = 0.6
fluid_press = 1.0
drag_coef = 0.5
friction_coef = 0.2
velocity_eps = 0.01
depth_eps = 0.0001
spread_eps = 1e-06
ghost_cells = 6

def minmod(first, second):
    return 0.5 * (jnp.sign(first) + jnp.sign(second)) * jnp.minimum(jnp.abs(first), jnp.abs(second))

def velocity(momentum, depth):
    return momentum * depth / (depth * depth + depth_eps)

def face_states(values, axis):
    cells = values.shape[axis]
    lower = lax.slice_in_dim(values, 0, cells - 2, axis=axis)
    middle = lax.slice_in_dim(values, 1, cells - 1, axis=axis)
    upper = lax.slice_in_dim(values, 2, cells, axis=axis)
    slopes = minmod(middle - lower, upper - middle)
    left_side = lax.slice_in_dim(middle + 0.5 * slopes, 0, cells - 3, axis=axis)
    right_side = lax.slice_in_dim(middle - 0.5 * slopes, 1, cells - 2, axis=axis)
    return (left_side, right_side)

def phase_flux(left_side, right_side, depth_index, normal_index, tangent_index, pressure):
    depth_left = left_side[depth_index]
    normal_left = left_side[normal_index]
    tangent_left = left_side[tangent_index]
    depth_right = right_side[depth_index]
    normal_right = right_side[normal_index]
    tangent_right = right_side[tangent_index]
    speed_left = velocity(normal_left, depth_left)
    speed_right = velocity(normal_right, depth_right)
    wave_left = jnp.sqrt(pressure * jnp.maximum(depth_left, 0.0))
    wave_right = jnp.sqrt(pressure * jnp.maximum(depth_right, 0.0))
    lowest = jnp.minimum(jnp.minimum(speed_left - wave_left, speed_right - wave_right), 0.0)
    highest = jnp.maximum(jnp.maximum(speed_left + wave_left, speed_right + wave_right), 0.0)
    flux_left = (normal_left, normal_left * speed_left + 0.5 * pressure * depth_left * depth_left, tangent_left * speed_left)
    flux_right = (normal_right, normal_right * speed_right + 0.5 * pressure * depth_right * depth_right, tangent_right * speed_right)
    jumps = (depth_right - depth_left, normal_right - normal_left, tangent_right - tangent_left)
    spread = highest - lowest + spread_eps
    return [(highest * fl - lowest * fr + lowest * highest * jump) / spread for fl, fr, jump in zip(flux_left, flux_right, jumps)]

def axis_flux(values, axis, normal_offset):
    left_side, right_side = face_states(values, axis)
    fields = [None] * 6
    for phase, pressure in ((0, solid_press), (1, fluid_press)):
        normal_index = 2 + 2 * phase + normal_offset
        tangent_index = 2 + 2 * phase + 1 - normal_offset
        parts_out = phase_flux(left_side, right_side, phase, normal_index, tangent_index, pressure)
        fields[phase] = parts_out[0]
        fields[normal_index] = parts_out[1]
        fields[tangent_index] = parts_out[2]
    return jnp.stack(fields)

def tendency(values, ground):
    row_flux = axis_flux(values, 1, 0)
    row_change = (row_flux[:, 1:, :] - row_flux[:, :-1, :])[:, :, 2:-2]
    col_flux = axis_flux(values, 2, 1)
    col_change = (col_flux[:, :, 1:] - col_flux[:, :, :-1])[:, 2:-2, :]
    inner = values[:, 2:-2, 2:-2]
    slope_rows = 0.5 * (ground[3:-1, 2:-2] - ground[1:-3, 2:-2])
    slope_cols = 0.5 * (ground[2:-2, 3:-1] - ground[2:-2, 1:-3])
    depth_solid = inner[0]
    depth_fluid = inner[1]
    solid_rows = velocity(inner[2], depth_solid)
    solid_cols = velocity(inner[3], depth_solid)
    fluid_rows = velocity(inner[4], depth_fluid)
    fluid_cols = velocity(inner[5], depth_fluid)
    coupling = drag_coef * depth_solid * depth_fluid / (jnp.abs(depth_solid) + jnp.abs(depth_fluid) + depth_eps)
    friction = friction_coef * depth_solid / jnp.sqrt(solid_rows * solid_rows + solid_cols * solid_cols + velocity_eps)
    zeros_field = jnp.zeros_like(depth_solid)
    sources = jnp.stack([zeros_field, zeros_field, -solid_press * depth_solid * slope_rows + coupling * (fluid_rows - solid_rows) - friction * solid_rows, -solid_press * depth_solid * slope_cols + coupling * (fluid_cols - solid_cols) - friction * solid_cols, -fluid_press * depth_fluid * slope_rows - coupling * (fluid_rows - solid_rows), -fluid_press * depth_fluid * slope_cols - coupling * (fluid_cols - solid_cols)])
    return sources - row_change - col_change

def advance(window):
    values = window[:6]
    ground = window[6]
    first = values[:, 2:-2, 2:-2] + time_step * tendency(values, ground)
    second = 0.75 * values[:, 4:-4, 4:-4] + 0.25 * (first[:, 2:-2, 2:-2] + time_step * tendency(first, ground[2:-2, 2:-2]))
    third = second[:, 2:-2, 2:-2] + time_step * tendency(second, ground[4:-4, 4:-4])
    return values[:, 6:-6, 6:-6] / 3.0 + 2.0 / 3.0 * third

def keep(window):
    return window[:6, 6:-6, 6:-6]

def reference(depths, momenta, bed, active):
    fields_now = jnp.concatenate([depths, momenta], axis=0)
    for outer_step in range(OUTER):
        stacked = jnp.concatenate([fields_now, bed[None]], axis=0)
        wrapped = jnp.pad(stacked, ((0, 0), (0, 0), (ghost_cells, ghost_cells)), mode='wrap')
        padded = jnp.pad(wrapped, ((0, 0), (ghost_cells, ghost_cells), (0, 0)), mode='edge')

        def column(column_index):
            block = lax.dynamic_slice_in_dim(padded, (column_index * PATCH).astype(jnp.int32), PATCH + 2 * ghost_cells, axis=2)
            pieces = []
            for slot_index in range(SLOTS):
                window = block[:, slot_index * PATCH:slot_index * PATCH + PATCH + 2 * ghost_cells, :]
                pieces.append(lax.cond(active[slot_index, column_index] > 0, advance, keep, window))
            return jnp.concatenate(pieces, axis=1)
        columns_out = lax.map(column, jnp.arange(COLUMNS, dtype=jnp.int32))
        fields_now = jnp.transpose(columns_out, (1, 2, 0, 3)).reshape(6, RAD, AROUND)
    return (fields_now[:2], fields_now[2:])
```

```python
import functools

import jax
import jax.numpy as jnp
from jax import lax
from jax.experimental import pallas as pl
from jax.experimental.pallas import tpu as pltpu
from jax.sharding import PartitionSpec as P

time_step = 0.04
solid_press = 0.6
fluid_press = 1.0
drag_coef = 0.5
friction_coef = 0.2
velocity_eps = 0.01
depth_eps = 0.0001
spread_eps = 1e-06
halo = 6
core_cols = 2 * halo
strip = 3 * halo
pair = 2 * strip
segments = 3
tiny = 1e-30

MESH = pl.DeviceIdType.MESH


def recip(x):
    return pl.reciprocal(x, approx=True)


def lanes(x, shift):
    shift = shift % x.shape[-1]
    return x if shift == 0 else pltpu.roll(x, shift, 1)


def minmod(a, b):
    return jnp.maximum(jnp.minimum(a, b), jnp.minimum(jnp.maximum(a, b), 0.0))


def wave(depth, pressure):
    x = pressure * depth
    return jnp.maximum(x, 0.0) * lax.rsqrt(jnp.maximum(x, tiny))


def hll(left, right, pressure):
    hl, ml, tl = left
    hr, mr, tr = right
    hl2 = hl * hl
    hr2 = hr * hr
    ul = ml * hl * recip(hl2 + depth_eps)
    ur = mr * hr * recip(hr2 + depth_eps)
    cl = wave(hl, pressure)
    cr = wave(hr, pressure)
    low = jnp.minimum(jnp.minimum(ul - cl, ur - cr), 0.0)
    high = jnp.maximum(jnp.maximum(ul + cl, ur + cr), 0.0)
    r = time_step * recip(high - low + spread_eps)
    a = high * r
    b = low * r
    c = a * low
    al = a * ul - c
    br = b * ur - c
    fh = a * ml - b * mr + c * (hr - hl)
    fn = al * ml - br * mr + (0.5 * pressure) * (a * hl2 - b * hr2)
    ft = al * tl - br * tr
    return fh, fn, ft


def both_phases(left, right, offset):
    out = [None] * 6
    for phase, pressure in ((0, solid_press), (1, fluid_press)):
        ids = (phase, 2 + 2 * phase + offset, 3 + 2 * phase - offset)
        parts = hll([left[i] for i in ids], [right[i] for i in ids], pressure)
        for i, part in zip(ids, parts):
            out[i] = part
    return out


def row_states(src, at):
    lefts, rights = [], []
    for f in range(6):
        v = src[f, pl.ds(at, 8), :]
        below = src[f, pl.ds(at - 1, 8), :]
        above = src[f, pl.ds(at + 1, 8), :]
        s = 0.5 * minmod(v - below, above - v)
        lefts.append(v + s)
        rights.append(v - s)
    return lefts, rights


def tendency(v, br, bc):
    lefts, rights = [], []
    for f in range(6):
        h = 0.5 * v[f]
        d = h - lanes(h, 1)
        s = minmod(d, lanes(d, -1))
        lefts.append(lanes(v[f] + s, 1))
        rights.append(v[f] - s)
    flux = both_phases(lefts, rights, 1)
    change = [lanes(x, -1) - x for x in flux]
    hs, hf = v[0], v[1]
    ws = hs * recip(hs * hs + depth_eps)
    wf = hf * recip(hf * hf + depth_eps)
    sr, sc, fr, fc = v[2] * ws, v[3] * ws, v[4] * wf, v[5] * wf
    drag = (time_step * drag_coef) * hs * hf * recip(jnp.abs(hs) + jnp.abs(hf) + depth_eps)
    rub = (time_step * friction_coef) * hs * lax.rsqrt(sr * sr + sc * sc + velocity_eps)
    dr = drag * (fr - sr)
    dc = drag * (fc - sc)
    ps = solid_press * hs
    pf = fluid_press * hf
    gains = [
        None,
        None,
        dr - ps * br - rub * sr,
        dc - ps * bc - rub * sc,
        dr + pf * br,
        dc + pf * bc,
    ]
    out = []
    for f in range(6):
        if f < 2:
            out.append(-change[f])
        elif f < 4:
            out.append(gains[f] - change[f])
        else:
            out.append(-gains[f] - change[f])
    return out


def run_stage(stage, src, start, beds, dst, first, count, unroll):
    row = lax.broadcasted_iota(jnp.int32, (8, 128), 0)
    top = row == 0
    bottom = row == 7

    def faces(at, carried):
        lefts, rights = row_states(src, at)
        rolled = [pltpu.roll(x, 1, 0) for x in lefts]
        shifted = [jnp.where(top, a, b) for a, b in zip(carried, rolled)]
        return both_phases(shifted, rights, 0), rolled

    at0 = first * 8
    lefts, _ = row_states(src, max(at0 - 8, 8))
    carried = [pltpu.roll(x, 1, 0) for x in lefts]
    flux, carried = faces(at0, carried)
    rolled_flux = [pltpu.roll(x, 7, 0) for x in flux]

    def one(at, carried, flux, rolled_flux):
        nxt, carried = faces(at + 8, carried)
        rolled_next = [pltpu.roll(x, 7, 0) for x in nxt]
        v = [src[f, pl.ds(at, 8), :] for f in range(6)]
        gain = tendency(v, beds[0, pl.ds(at, 8), :], beds[1, pl.ds(at, 8), :])
        for f in range(6):
            up = jnp.where(bottom, rolled_next[f], rolled_flux[f])
            new = v[f] + (gain[f] - (up - flux[f]))
            if stage == 1:
                new = 0.75 * start[f, pl.ds(at, 8), :] + 0.25 * new
            elif stage == 2:
                new = (1.0 / 3.0) * start[f, pl.ds(at, 8), :] + (2.0 / 3.0) * new
            dst[f, pl.ds(at, 8), :] = new
        return carried, nxt, rolled_next

    def body(i, state):
        carried, flux, rolled_flux = state
        base = pl.multiple_of(at0 + i * (8 * unroll), 8)
        for u in range(unroll):
            carried, flux, rolled_flux = one(base + 8 * u, carried, flux, rolled_flux)
        return carried, flux, rolled_flux

    lax.fori_loop(0, count // unroll, body, (carried, flux, rolled_flux))


def bed_slopes(x, beds, first, count):
    def body(i, carry):
        at = pl.multiple_of((first + i) * 8, 8)
        b = x[6, pl.ds(at, 8), :]
        beds[0, pl.ds(at, 8), :] = (0.5 * time_step) * (
            x[6, pl.ds(at + 1, 8), :] - x[6, pl.ds(at - 1, 8), :]
        )
        beds[1, pl.ds(at, 8), :] = (0.5 * time_step) * (lanes(b, -1) - lanes(b, 1))
        return carry

    lax.fori_loop(0, count, body, 0)


def kernel(count, rows, depths, momenta, bed, active, out_d, out_m,
           x, beds, one, two, sx, sbeds, sone, stwo, send, recv, send_sem, recv_sem):
    me = lax.axis_index("patch")
    right, left = lax.rem(me + 1, count), lax.rem(me + count - 1, count)
    barrier = pltpu.get_barrier_semaphore()
    for other in (left, right):
        pl.semaphore_signal(barrier, inc=1, device_id={"patch": other}, device_id_type=MESH)

    lane = lax.broadcasted_iota(jnp.int32, (8, 128), 1)
    groups = rows // 8
    step = 40
    strip_groups = 8
    end = 16 + rows

    for f in range(7):
        own = depths.at[f] if f < 2 else momenta.at[f - 2] if f < 6 else bed
        x[f, 16:end, :] = own[...]
        x[f, 0:16, :] = jnp.broadcast_to(own[0:1, :], (16, 128))
        x[f, end : end + 24, :] = jnp.broadcast_to(own[rows - 1 : rows, :], (24, 128))

    def pack(q, carry):
        to_left = jnp.zeros((8, 128), jnp.float32)
        to_right = jnp.zeros((8, 128), jnp.float32)
        for f in range(7):
            for s in range(segments):
                v = x[f, pl.ds(pl.multiple_of(8 + step * s + 8 * q, 8), 8), :]
                at = strip * f + halo * s
                here = (lane >= at) & (lane < at + halo)
                to_left = jnp.where(here, lanes(v, at), to_left)
                to_right = jnp.where(here, lanes(v, at - (128 - halo)), to_right)
        rows_q = pl.ds(pl.multiple_of(8 * q, 8), 8)
        send[0, rows_q, :] = to_left
        send[1, rows_q, :] = to_right
        return carry

    lax.fori_loop(0, strip_groups, pack, 0)

    pl.semaphore_wait(barrier, 2)
    copies = []
    for i, other in ((0, left), (1, right)):
        copy = pltpu.make_async_remote_copy(
            src_ref=send.at[i],
            dst_ref=recv.at[i],
            send_sem=send_sem.at[i],
            recv_sem=recv_sem.at[i],
            device_id={"patch": other},
            device_id_type=MESH,
        )
        copy.start()
        copies.append(copy)

    bed_slopes(x, beds, 1, groups + 2)
    run_stage(0, x, x, beds, one, 1, groups + 2, 2)
    run_stage(1, one, x, beds, two, 1, groups + 2, 2)
    run_stage(2, two, x, beds, one, 2, groups, 2)

    for copy in copies:
        copy.wait()

    def gather(q, carry):
        rows_q = pl.ds(pl.multiple_of(8 * q, 8), 8)
        from_right = recv[0, rows_q, :]
        from_left = recv[1, rows_q, :]
        dest = pl.ds(pl.multiple_of(8 + 8 * q, 8), 8)
        for f in range(7):
            acc = jnp.zeros((8, 128), jnp.float32)
            for s in range(segments):
                v = x[f, pl.ds(pl.multiple_of(8 + step * s + 8 * q, 8), 8), :]
                at = strip * f + halo * s
                base = pair * s
                pieces = (
                    (lanes(v, base - (128 - core_cols)), base, core_cols),
                    (lanes(from_right, base + core_cols - at), base + core_cols, halo),
                    (lanes(from_left, base + strip - at), base + strip, halo),
                    (lanes(v, base + strip + halo), base + strip + halo, core_cols),
                )
                for moved, begin, width in pieces:
                    acc = jnp.where((lane >= begin) & (lane < begin + width), moved, acc)
            sx[f, dest, :] = acc
        return carry

    lax.fori_loop(0, strip_groups, gather, 0)
    for f in range(7):
        sx[f, 0:8, :] = sx[f, 8:16, :]
        sx[f, 72:88, :] = sx[f, 56:72, :]

    bed_slopes(sx, sbeds, 1, strip_groups)
    run_stage(0, sx, sx, sbeds, sone, 1, strip_groups, 2)
    run_stage(1, sone, sx, sbeds, stwo, 1, strip_groups, 2)
    run_stage(2, stwo, sx, sbeds, sone, 2, strip_groups - 2, 2)

    live = jnp.broadcast_to(active[...], (8, 128)) > 0
    left_edge = lane < halo
    right_edge = lane >= 128 - halo

    def merge(s, begin):
        def body(q, carry):
            strip_at = pl.multiple_of(8 * q, 8)
            row_at = pl.multiple_of(8 * q + (step * s - 16), 8)
            for f in range(6):
                e = sone[f, pl.ds(strip_at, 8), :]
                new = one[f, pl.ds(row_at + 16, 8), :]
                new = jnp.where(left_edge, lanes(e, -(pair * s + strip + halo)), new)
                new = jnp.where(right_edge, lanes(e, 128 - halo - (pair * s + halo)), new)
                new = jnp.where(live, new, x[f, pl.ds(row_at + 16, 8), :])
                if f < 2:
                    out_d[f, pl.ds(row_at, 8), :] = new
                else:
                    out_m[f - 2, pl.ds(row_at, 8), :] = new
            return carry

        lax.fori_loop(begin, strip_groups, body, 0)

    merge(0, 2)
    merge(1, 3)
    merge(2, 3)


def per_device(depths, momenta, bed, active):
    rows, cols = bed.shape
    count = lax.axis_size("patch")
    tall = rows + 40
    f32 = jnp.float32
    vmem = pl.BlockSpec(memory_space=pltpu.VMEM)
    return pl.pallas_call(
        functools.partial(kernel, count, rows),
        out_shape=(
            jax.ShapeDtypeStruct(depths.shape, f32),
            jax.ShapeDtypeStruct(momenta.shape, f32),
        ),
        in_specs=[vmem] * 4,
        out_specs=(vmem, vmem),
        scratch_shapes=[
            pltpu.VMEM((7, tall, cols), f32),
            pltpu.VMEM((2, tall, cols), f32),
            pltpu.VMEM((6, tall, cols), f32),
            pltpu.VMEM((6, tall, cols), f32),
            pltpu.VMEM((7, 88, cols), f32),
            pltpu.VMEM((2, 88, cols), f32),
            pltpu.VMEM((6, 88, cols), f32),
            pltpu.VMEM((6, 88, cols), f32),
            pltpu.VMEM((2, 64, cols), f32),
            pltpu.VMEM((2, 64, cols), f32),
            pltpu.SemaphoreType.DMA((2,)),
            pltpu.SemaphoreType.DMA((2,)),
        ],
        compiler_params=pltpu.CompilerParams(
            collective_id=0, has_side_effects=True, vmem_limit_bytes=32 * 1024 * 1024
        ),
    )(depths, momenta, bed, active)


def solution(mesh):
    placed = (
        P(None, None, ("runs", "patch")),
        P(None, None, ("runs", "patch")),
        P(None, ("runs", "patch")),
        P(None, ("runs", "patch")),
    )
    return jax.shard_map(
        per_device,
        mesh=mesh,
        in_specs=placed,
        out_specs=(P(None, None, ("runs", "patch")), P(None, None, ("runs", "patch"))),
        check_vma=False,
    )
```

```python
import functools

import jax
import jax.numpy as jnp
from jax import lax
from jax.experimental import pallas as pl
from jax.experimental.pallas import tpu as pltpu
from jax.sharding import PartitionSpec as P

time_step = 0.04
solid_press = 0.6
fluid_press = 1.0
drag_coef = 0.5
friction_coef = 0.2
velocity_eps = 0.01
depth_eps = 0.0001
spread_eps = 1e-06
halo = 6
core_cols = 2 * halo
strip = 3 * halo
pair = 2 * strip
segments = 3
tiny = 1e-30
unroll = 9
step = 40
strip_groups = 8

MESH = pl.DeviceIdType.MESH


def recip(x):
    return pl.reciprocal(x, approx=True)


def lanes(x, shift):
    shift = shift % x.shape[-1]
    return x if shift == 0 else pltpu.roll(x, shift, 1)


def minmod(a, b):
    return jnp.maximum(jnp.minimum(a, b), jnp.minimum(jnp.maximum(a, b), 0.0))


def wave(depth, pressure):
    x = pressure * depth
    return jnp.maximum(x, 0.0) * lax.rsqrt(jnp.maximum(x, tiny))


def hll(left, right, pressure):
    hl, ml, tl = left
    hr, mr, tr = right
    hl2 = hl * hl
    hr2 = hr * hr
    ul = ml * hl * recip(hl2 + depth_eps)
    ur = mr * hr * recip(hr2 + depth_eps)
    cl = wave(hl, pressure)
    cr = wave(hr, pressure)
    low = jnp.minimum(jnp.minimum(ul - cl, ur - cr), 0.0)
    high = jnp.maximum(jnp.maximum(ul + cl, ur + cr), 0.0)
    r = time_step * recip(high - low + spread_eps)
    a = high * r
    b = low * r
    c = a * low
    al = a * ul - c
    br = b * ur - c
    fh = a * ml - b * mr + c * (hr - hl)
    fn = al * ml - br * mr + (0.5 * pressure) * (a * hl2 - b * hr2)
    ft = al * tl - br * tr
    return fh, fn, ft


def both_phases(left, right, offset):
    out = [None] * 6
    for phase, pressure in ((0, solid_press), (1, fluid_press)):
        ids = (phase, 2 + 2 * phase + offset, 3 + 2 * phase - offset)
        parts = hll([left[i] for i in ids], [right[i] for i in ids], pressure)
        for i, part in zip(ids, parts):
            out[i] = part
    return out


def row_states(src, at):
    lefts, rights = [], []
    for f in range(6):
        v = src[f, pl.ds(at, 8), :]
        below = src[f, pl.ds(at - 1, 8), :]
        above = src[f, pl.ds(at + 1, 8), :]
        s = 0.5 * minmod(v - below, above - v)
        lefts.append(v + s)
        rights.append(v - s)
    return lefts, rights


def tendency(v, br, bc):
    lefts, rights = [], []
    for f in range(6):
        h = 0.5 * v[f]
        d = h - lanes(h, 1)
        s = minmod(d, lanes(h, -1) - h)
        lefts.append(lanes(v[f] + s, 1))
        rights.append(v[f] - s)
    flux = both_phases(lefts, rights, 1)
    change = [lanes(x, -1) - x for x in flux]
    hs, hf = v[0], v[1]
    ws = hs * recip(hs * hs + depth_eps)
    wf = hf * recip(hf * hf + depth_eps)
    sr, sc, fr, fc = v[2] * ws, v[3] * ws, v[4] * wf, v[5] * wf
    drag = (time_step * drag_coef) * hs * hf * recip(jnp.abs(hs) + jnp.abs(hf) + depth_eps)
    rub = (time_step * friction_coef) * hs * lax.rsqrt(sr * sr + sc * sc + velocity_eps)
    dr = drag * (fr - sr)
    dc = drag * (fc - sc)
    ps = solid_press * hs
    pf = fluid_press * hf
    gains = [
        None,
        None,
        dr - ps * br - rub * sr,
        dc - ps * bc - rub * sc,
        dr + pf * br,
        dc + pf * bc,
    ]
    out = []
    for f in range(6):
        if f < 2:
            out.append(-change[f])
        elif f < 4:
            out.append(gains[f] - change[f])
        else:
            out.append(-gains[f] - change[f])
    return out


def run_stage(stage, buf, bed, at0, trips):
    src = buf.at[stage]
    dst = buf.at[stage + 1]
    old_part, new_part = ((0.0, 1.0), (0.75, 0.25), (1.0 / 3.0, 2.0 / 3.0))[stage]
    row = lax.broadcasted_iota(jnp.int32, (8, 128), 0)
    top = row == 0
    bottom = row == 7

    def faces(at, carried):
        lefts, rights = row_states(src, at)
        rolled = [pltpu.roll(x, 1, 0) for x in lefts]
        shifted = [jnp.where(top, a, b) for a, b in zip(carried, rolled)]
        return both_phases(shifted, rights, 0), rolled

    def one(at, carried, flux, rolled_flux):
        nxt, carried = faces(at + 8, carried)
        rolled_next = [pltpu.roll(x, 7, 0) for x in nxt]
        v = [src[f, pl.ds(at, 8), :] for f in range(6)]
        b = bed[pl.ds(at, 8), :]
        bed_r = (0.5 * time_step) * (bed[pl.ds(at + 1, 8), :] - bed[pl.ds(at - 1, 8), :])
        bed_c = (0.5 * time_step) * (lanes(b, -1) - lanes(b, 1))
        gain = tendency(v, bed_r, bed_c)
        for f in range(6):
            up = jnp.where(bottom, rolled_next[f], rolled_flux[f])
            new = v[f] + (gain[f] - (up - flux[f]))
            if stage:
                new = old_part * buf[0, f, pl.ds(at, 8), :] + new_part * new
            dst[f, pl.ds(at, 8), :] = new
        return carried, nxt, rolled_next

    def body(i, state):
        carried, flux, rolled_flux = state
        base = pl.multiple_of(at0 + i * (8 * unroll), 8)
        for u in range(unroll):
            carried, flux, rolled_flux = one(base + 8 * u, carried, flux, rolled_flux)
        return carried, flux, rolled_flux

    carried = [jnp.zeros((8, 128), jnp.float32)] * 6
    flux, carried = faces(at0, carried)
    rolled_flux = [pltpu.roll(x, 7, 0) for x in flux]
    lax.fori_loop(0, trips, body, (carried, flux, rolled_flux))


def kernel(count, rows, depths, momenta, bed_in, active, out_d, out_m,
           buf, bed, send, recv, load_sem, send_sem, recv_sem):
    me = lax.axis_index("patch")
    right, left = lax.rem(me + 1, count), lax.rem(me + count - 1, count)
    barrier = pltpu.get_barrier_semaphore()
    for other in (left, right):
        pl.semaphore_signal(barrier, inc=1, device_id={"patch": other}, device_id_type=MESH)

    end = 16 + rows
    loads = [
        pltpu.make_async_copy(depths, buf.at[0, 0:2, 16:end], load_sem.at[0]),
        pltpu.make_async_copy(momenta, buf.at[0, 2:6, 16:end], load_sem.at[1]),
        pltpu.make_async_copy(bed_in, bed.at[16:end], load_sem.at[2]),
    ]
    for load in loads:
        load.start()

    lane = lax.broadcasted_iota(jnp.int32, (8, 128), 1)
    strip0 = rows + 40
    fields = [buf.at[0, f] for f in range(6)] + [bed]
    for load in loads:
        load.wait()
    for x in fields:
        x[0:16, :] = jnp.broadcast_to(x[16:17, :], (16, 128))
        x[end : end + 24, :] = jnp.broadcast_to(x[end - 1 : end, :], (24, 128))

    def pack(q, carry):
        to_left = jnp.zeros((8, 128), jnp.float32)
        to_right = jnp.zeros((8, 128), jnp.float32)
        for f in range(7):
            for s in range(segments):
                v = fields[f][pl.ds(pl.multiple_of(8 + step * s + 8 * q, 8), 8), :]
                at = pair * s + halo * f if f < 6 else pair * segments + halo * s
                here = (lane >= at) & (lane < at + halo)
                to_left = jnp.where(here, lanes(v, at), to_left)
                to_right = jnp.where(here, lanes(v, at - (128 - halo)), to_right)
        rows_q = pl.ds(pl.multiple_of(8 * q, 8), 8)
        send[0, rows_q, :] = to_left
        send[1, rows_q, :] = to_right
        return carry

    lax.fori_loop(0, strip_groups, pack, 0, unroll=4)

    pl.semaphore_wait(barrier, 2)
    copies = []
    for i, other in ((0, left), (1, right)):
        copy = pltpu.make_async_remote_copy(
            src_ref=send.at[i],
            dst_ref=recv.at[i],
            send_sem=send_sem.at[i],
            recv_sem=recv_sem.at[i],
            device_id={"patch": other},
            device_id_type=MESH,
        )
        copy.start()
        copies.append(copy)

    def own_columns(q, carry):
        dest = pl.ds(pl.multiple_of(strip0 + 8 + 8 * q, 8), 8)
        for f in range(7):
            acc = jnp.zeros((8, 128), jnp.float32)
            for s in range(segments):
                v = fields[f][pl.ds(pl.multiple_of(8 + step * s + 8 * q, 8), 8), :]
                base = pair * s
                here = (lane >= base) & (lane < base + core_cols)
                acc = jnp.where(here, lanes(v, base - (128 - core_cols)), acc)
                base = base + strip + halo
                here = (lane >= base) & (lane < base + core_cols)
                acc = jnp.where(here, lanes(v, base), acc)
            fields[f][dest, :] = acc
        return carry

    lax.fori_loop(0, strip_groups, own_columns, 0, unroll=2)

    def within(begins, width):
        here = None
        for begin in begins:
            one = (lane >= begin) & (lane < begin + width)
            here = one if here is None else here | one
        return here

    starts = [pair * s for s in range(segments)]

    def halo_columns():
        sides = []
        for i, offset in ((0, core_cols), (1, strip)):
            sides.append((i, offset, within([b + offset for b in starts], halo)))
        for q in range(strip_groups):
            dest = pl.ds(strip0 + 8 + 8 * q, 8)
            got = [recv[i, 8 * q : 8 * q + 8, :] for i in range(2)]
            for f in range(7):
                acc = fields[f][dest, :]
                for i, offset, here in sides:
                    if f < 6:
                        acc = jnp.where(here, lanes(got[i], offset - halo * f), acc)
                    else:
                        for s in range(segments):
                            begin = pair * s + offset
                            moved = lanes(got[i], begin - (pair * segments + halo * s))
                            acc = jnp.where(within([begin], halo), moved, acc)
                fields[f][dest, :] = acc

    def tile(t, carry):
        @pl.when(t == 1)
        def _():
            for copy in copies:
                copy.wait()
            halo_columns()
            for x in fields:
                x[strip0 : strip0 + 8, :] = x[strip0 + 8 : strip0 + 16, :]
                x[strip0 + 72 : strip0 + 96, :] = x[strip0 + 48 : strip0 + 72, :]

        at0 = pl.multiple_of(8 + t * strip0, 8)
        trips = jnp.where(t == 0, (rows // 8 + 1 + unroll) // unroll, (strip_groups - 1 + unroll) // unroll)

        def stage_body(stage, carry):
            run_stage(stage, buf, bed, at0, trips)
            return carry

        for stage in range(3):
            run_stage(stage, buf, bed, at0, trips)
        return carry

    lax.fori_loop(0, 2, tile, 0)

    live = jnp.broadcast_to(active[...], (8, 128)) > 0
    left_edge = lane < halo
    right_edge = lane >= 128 - halo

    def merge(s, begin):
        for q in range(begin, strip_groups):
            row_at = 8 * q + step * s - 16
            for f in range(6):
                e = buf[3, f, strip0 + 8 * q : strip0 + 8 * q + 8, :]
                new = buf[3, f, row_at + 16 : row_at + 24, :]
                new = jnp.where(left_edge, lanes(e, -(pair * s + strip + halo)), new)
                new = jnp.where(right_edge, lanes(e, 128 - halo - (pair * s + halo)), new)
                new = jnp.where(live, new, buf[0, f, row_at + 16 : row_at + 24, :])
                if f < 2:
                    out_d[f, row_at : row_at + 8, :] = new
                else:
                    out_m[f - 2, row_at : row_at + 8, :] = new

    merge(0, 2)
    merge(1, 3)
    merge(2, 3)


def per_device(depths, momenta, bed, active):
    rows, cols = bed.shape
    count = lax.axis_size("patch")
    tall = rows + 40 + 96
    f32 = jnp.float32
    vmem = pl.BlockSpec(memory_space=pltpu.VMEM)
    hbm = pl.BlockSpec(memory_space=pltpu.HBM)
    return pl.pallas_call(
        functools.partial(kernel, count, rows),
        out_shape=(
            jax.ShapeDtypeStruct(depths.shape, f32),
            jax.ShapeDtypeStruct(momenta.shape, f32),
        ),
        in_specs=[hbm, hbm, hbm, vmem],
        out_specs=(vmem, vmem),
        scratch_shapes=[
            pltpu.VMEM((4, 6, tall, cols), f32),
            pltpu.VMEM((tall, cols), f32),
            pltpu.VMEM((2, 64, cols), f32),
            pltpu.VMEM((2, 64, cols), f32),
            pltpu.SemaphoreType.DMA((3,)),
            pltpu.SemaphoreType.DMA((2,)),
            pltpu.SemaphoreType.DMA((2,)),
        ],
        compiler_params=pltpu.CompilerParams(
            collective_id=0, has_side_effects=True, vmem_limit_bytes=32 * 1024 * 1024
        ),
    )(depths, momenta, bed, active)


def solution(mesh):
    placed = (
        P(None, None, ("runs", "patch")),
        P(None, None, ("runs", "patch")),
        P(None, ("runs", "patch")),
        P(None, ("runs", "patch")),
    )
    return jax.shard_map(
        per_device,
        mesh=mesh,
        in_specs=placed,
        out_specs=(P(None, None, ("runs", "patch")), P(None, None, ("runs", "patch"))),
        check_vma=False,
    )
```

```python
import functools

import jax
import jax.numpy as jnp
from jax import lax
from jax.experimental import pallas as pl
from jax.experimental.pallas import tpu as pltpu
from jax.sharding import PartitionSpec as P

time_step = 0.04
solid_press = 0.6
fluid_press = 1.0
drag_coef = 0.5
friction_coef = 0.2
velocity_eps = 0.01
depth_eps = 0.0001
spread_eps = 1e-06
halo = 6
core_cols = 2 * halo
strip = 3 * halo
pair = 2 * strip
segments = 3
tiny = 1e-30
unroll = 9
step = 40
strip_groups = 8
send_after = 0

MESH = pl.DeviceIdType.MESH


def recip(x):
    return pl.reciprocal(x, approx=True)


def lanes(x, shift):
    shift = shift % x.shape[-1]
    return x if shift == 0 else pltpu.roll(x, shift, 1)


def minmod(a, b):
    return jnp.maximum(jnp.minimum(a, b), jnp.minimum(jnp.maximum(a, b), 0.0))


def wave(depth, pressure):
    x = pressure * depth
    return jnp.maximum(x, 0.0) * lax.rsqrt(jnp.maximum(x, tiny))


def hll(left, right, pressure):
    hl, ml, tl = left
    hr, mr, tr = right
    hl2 = hl * hl
    hr2 = hr * hr
    ul = ml * hl * recip(hl2 + depth_eps)
    ur = mr * hr * recip(hr2 + depth_eps)
    cl = wave(hl, pressure)
    cr = wave(hr, pressure)
    low = jnp.minimum(jnp.minimum(ul - cl, ur - cr), 0.0)
    high = jnp.maximum(jnp.maximum(ul + cl, ur + cr), 0.0)
    r = time_step * recip(high - low + spread_eps)
    a = high * r
    b = low * r
    c = a * low
    al = a * ul - c
    br = b * ur - c
    fh = a * ml - b * mr + c * (hr - hl)
    fn = al * ml - br * mr + (0.5 * pressure) * (a * hl2 - b * hr2)
    ft = al * tl - br * tr
    return fh, fn, ft


def both_phases(left, right, offset):
    out = [None] * 6
    for phase, pressure in ((0, solid_press), (1, fluid_press)):
        ids = (phase, 2 + 2 * phase + offset, 3 + 2 * phase - offset)
        parts = hll([left[i] for i in ids], [right[i] for i in ids], pressure)
        for i, part in zip(ids, parts):
            out[i] = part
    return out


def row_states(src, at):
    lefts, rights = [], []
    for f in range(6):
        v = src[f, pl.ds(at, 8), :]
        below = src[f, pl.ds(at - 1, 8), :]
        above = src[f, pl.ds(at + 1, 8), :]
        s = 0.5 * minmod(v - below, above - v)
        lefts.append(v + s)
        rights.append(v - s)
    return lefts, rights


def tendency(v, br, bc):
    lefts, rights = [], []
    for f in range(6):
        h = 0.5 * v[f]
        d = h - lanes(h, 1)
        s = minmod(d, lanes(h, -1) - h)
        lefts.append(lanes(v[f] + s, 1))
        rights.append(v[f] - s)
    flux = both_phases(lefts, rights, 1)
    change = [lanes(x, -1) - x for x in flux]
    hs, hf = v[0], v[1]
    ws = hs * recip(hs * hs + depth_eps)
    wf = hf * recip(hf * hf + depth_eps)
    sr, sc, fr, fc = v[2] * ws, v[3] * ws, v[4] * wf, v[5] * wf
    drag = (time_step * drag_coef) * hs * hf * recip(jnp.abs(hs) + jnp.abs(hf) + depth_eps)
    rub = (time_step * friction_coef) * hs * lax.rsqrt(sr * sr + sc * sc + velocity_eps)
    dr = drag * (fr - sr)
    dc = drag * (fc - sc)
    ps = solid_press * hs
    pf = fluid_press * hf
    gains = [
        None,
        None,
        dr - ps * br - rub * sr,
        dc - ps * bc - rub * sc,
        dr + pf * br,
        dc + pf * bc,
    ]
    out = []
    for f in range(6):
        if f < 2:
            out.append(-change[f])
        elif f < 4:
            out.append(gains[f] - change[f])
        else:
            out.append(-gains[f] - change[f])
    return out


def run_stage(stage, buf, bed, at0, trips):
    src = buf.at[stage]
    dst = buf.at[stage + 1]
    old_part, new_part = ((0.0, 1.0), (0.75, 0.25), (1.0 / 3.0, 2.0 / 3.0))[stage]
    row = lax.broadcasted_iota(jnp.int32, (8, 128), 0)
    top = row == 0
    bottom = row == 7

    def faces(at, carried):
        lefts, rights = row_states(src, at)
        rolled = [pltpu.roll(x, 1, 0) for x in lefts]
        shifted = [jnp.where(top, a, b) for a, b in zip(carried, rolled)]
        return both_phases(shifted, rights, 0), rolled

    def one(at, carried, flux, rolled_flux):
        nxt, carried = faces(at + 8, carried)
        rolled_next = [pltpu.roll(x, 7, 0) for x in nxt]
        v = [src[f, pl.ds(at, 8), :] for f in range(6)]
        b = bed[pl.ds(at, 8), :]
        bed_r = (0.5 * time_step) * (bed[pl.ds(at + 1, 8), :] - bed[pl.ds(at - 1, 8), :])
        bed_c = (0.5 * time_step) * (lanes(b, -1) - lanes(b, 1))
        gain = tendency(v, bed_r, bed_c)
        for f in range(6):
            up = jnp.where(bottom, rolled_next[f], rolled_flux[f])
            new = v[f] + (gain[f] - (up - flux[f]))
            if stage:
                new = old_part * buf[0, f, pl.ds(at, 8), :] + new_part * new
            dst[f, pl.ds(at, 8), :] = new
        return carried, nxt, rolled_next

    def body(i, state):
        carried, flux, rolled_flux = state
        base = pl.multiple_of(at0 + i * (8 * unroll), 8)
        for u in range(unroll):
            carried, flux, rolled_flux = one(base + 8 * u, carried, flux, rolled_flux)
        return carried, flux, rolled_flux

    carried = [jnp.zeros((8, 128), jnp.float32)] * 6
    flux, carried = faces(at0, carried)
    rolled_flux = [pltpu.roll(x, 7, 0) for x in flux]
    lax.fori_loop(0, trips, body, (carried, flux, rolled_flux))


def kernel(count, rows, depths, momenta, bed_in, active, out_d, out_m,
           buf, bed, send, recv, load_sem, send_sem, recv_sem):
    me = lax.axis_index("patch")
    right, left = lax.rem(me + 1, count), lax.rem(me + count - 1, count)
    barrier = pltpu.get_barrier_semaphore()
    for other in (left, right):
        pl.semaphore_signal(barrier, inc=1, device_id={"patch": other}, device_id_type=MESH)

    end = 16 + rows
    loads = [
        pltpu.make_async_copy(depths, buf.at[0, 0:2, 16:end], load_sem.at[0]),
        pltpu.make_async_copy(momenta, buf.at[0, 2:6, 16:end], load_sem.at[1]),
        pltpu.make_async_copy(bed_in, bed.at[16:end], load_sem.at[2]),
    ]
    for load in loads:
        load.start()

    lane = lax.broadcasted_iota(jnp.int32, (8, 128), 1)
    strip0 = rows + 40
    fields = [buf.at[0, f] for f in range(6)] + [bed]
    for load in loads:
        load.wait()
    for x in fields:
        x[0:16, :] = jnp.broadcast_to(x[16:17, :], (16, 128))
        x[end : end + 24, :] = jnp.broadcast_to(x[end - 1 : end, :], (24, 128))

    def pack(q, carry):
        to_left = jnp.zeros((8, 128), jnp.float32)
        to_right = jnp.zeros((8, 128), jnp.float32)
        for f in range(7):
            for s in range(segments):
                v = fields[f][pl.ds(pl.multiple_of(8 + step * s + 8 * q, 8), 8), :]
                at = pair * s + halo * f if f < 6 else pair * segments + halo * s
                here = (lane >= at) & (lane < at + halo)
                to_left = jnp.where(here, lanes(v, at), to_left)
                to_right = jnp.where(here, lanes(v, at - (128 - halo)), to_right)
        rows_q = pl.ds(pl.multiple_of(8 * q, 8), 8)
        send[0, rows_q, :] = to_left
        send[1, rows_q, :] = to_right
        return carry

    lax.fori_loop(0, strip_groups, pack, 0, unroll=4)

    copies = [
        pltpu.make_async_remote_copy(
            src_ref=send.at[i],
            dst_ref=recv.at[i],
            send_sem=send_sem.at[i],
            recv_sem=recv_sem.at[i],
            device_id={"patch": other},
            device_id_type=MESH,
        )
        for i, other in ((0, left), (1, right))
    ]

    def own_columns(q, carry):
        dest = pl.ds(pl.multiple_of(strip0 + 8 + 8 * q, 8), 8)
        for f in range(7):
            acc = jnp.zeros((8, 128), jnp.float32)
            for s in range(segments):
                v = fields[f][pl.ds(pl.multiple_of(8 + step * s + 8 * q, 8), 8), :]
                base = pair * s
                here = (lane >= base) & (lane < base + core_cols)
                acc = jnp.where(here, lanes(v, base - (128 - core_cols)), acc)
                base = base + strip + halo
                here = (lane >= base) & (lane < base + core_cols)
                acc = jnp.where(here, lanes(v, base), acc)
            fields[f][dest, :] = acc
        return carry

    lax.fori_loop(0, strip_groups, own_columns, 0, unroll=2)

    def within(begins, width):
        here = None
        for begin in begins:
            one = (lane >= begin) & (lane < begin + width)
            here = one if here is None else here | one
        return here

    starts = [pair * s for s in range(segments)]

    def halo_columns():
        sides = []
        for i, offset in ((0, core_cols), (1, strip)):
            sides.append((i, offset, within([b + offset for b in starts], halo)))
        for q in range(strip_groups):
            dest = pl.ds(strip0 + 8 + 8 * q, 8)
            got = [recv[i, 8 * q : 8 * q + 8, :] for i in range(2)]
            for f in range(7):
                acc = fields[f][dest, :]
                for i, offset, here in sides:
                    if f < 6:
                        acc = jnp.where(here, lanes(got[i], offset - halo * f), acc)
                    else:
                        for s in range(segments):
                            begin = pair * s + offset
                            moved = lanes(got[i], begin - (pair * segments + halo * s))
                            acc = jnp.where(within([begin], halo), moved, acc)
                fields[f][dest, :] = acc

    def tile(t, carry):
        @pl.when(t == 1)
        def _():
            for copy in copies:
                copy.wait()
            halo_columns()
            for x in fields:
                x[strip0 : strip0 + 8, :] = x[strip0 + 8 : strip0 + 16, :]
                x[strip0 + 72 : strip0 + 96, :] = x[strip0 + 48 : strip0 + 72, :]

        at0 = pl.multiple_of(8 + t * strip0, 8)
        trips = jnp.where(t == 0, (rows // 8 + 1 + unroll) // unroll, (strip_groups - 1 + unroll) // unroll)

        for stage in range(3):
            run_stage(stage, buf, bed, at0, trips)
            if stage == send_after:

                @pl.when(t == 0)
                def _():
                    pl.semaphore_wait(barrier, 2)
                    for copy in copies:
                        copy.start()

        return carry

    lax.fori_loop(0, 2, tile, 0)

    live = jnp.broadcast_to(active[...], (8, 128)) > 0
    left_edge = lane < halo
    right_edge = lane >= 128 - halo

    def merge(s, begin):
        for q in range(begin, strip_groups):
            row_at = 8 * q + step * s - 16
            for f in range(6):
                e = buf[3, f, strip0 + 8 * q : strip0 + 8 * q + 8, :]
                new = buf[3, f, row_at + 16 : row_at + 24, :]
                new = jnp.where(left_edge, lanes(e, -(pair * s + strip + halo)), new)
                new = jnp.where(right_edge, lanes(e, 128 - halo - (pair * s + halo)), new)
                new = jnp.where(live, new, buf[0, f, row_at + 16 : row_at + 24, :])
                if f < 2:
                    out_d[f, row_at : row_at + 8, :] = new
                else:
                    out_m[f - 2, row_at : row_at + 8, :] = new

    merge(0, 2)
    merge(1, 3)
    merge(2, 3)


def per_device(depths, momenta, bed, active):
    rows, cols = bed.shape
    count = lax.axis_size("patch")
    tall = rows + 40 + 96
    f32 = jnp.float32
    vmem = pl.BlockSpec(memory_space=pltpu.VMEM)
    hbm = pl.BlockSpec(memory_space=pltpu.HBM)
    return pl.pallas_call(
        functools.partial(kernel, count, rows),
        out_shape=(
            jax.ShapeDtypeStruct(depths.shape, f32),
            jax.ShapeDtypeStruct(momenta.shape, f32),
        ),
        in_specs=[hbm, hbm, hbm, vmem],
        out_specs=(vmem, vmem),
        scratch_shapes=[
            pltpu.VMEM((4, 6, tall, cols), f32),
            pltpu.VMEM((tall, cols), f32),
            pltpu.VMEM((2, 64, cols), f32),
            pltpu.VMEM((2, 64, cols), f32),
            pltpu.SemaphoreType.DMA((3,)),
            pltpu.SemaphoreType.DMA((2,)),
            pltpu.SemaphoreType.DMA((2,)),
        ],
        compiler_params=pltpu.CompilerParams(
            collective_id=0, has_side_effects=True, vmem_limit_bytes=32 * 1024 * 1024
        ),
    )(depths, momenta, bed, active)


def solution(mesh):
    placed = (
        P(None, None, ("runs", "patch")),
        P(None, None, ("runs", "patch")),
        P(None, ("runs", "patch")),
        P(None, ("runs", "patch")),
    )
    return jax.shard_map(
        per_device,
        mesh=mesh,
        in_specs=placed,
        out_specs=(P(None, None, ("runs", "patch")), P(None, None, ("runs", "patch"))),
        check_vma=False,
    )
```
